32 devices in a mesh: groups: 2 (over x), branch: 16 (over z, y, core).
Axes of the slice: x: 2, y: 2, z: 4, core: 2. Of those that a mesh axis runs over, the one named last changes fastest.
Arguments:
- xbc: bfloat16 [8192, 8448], P(('groups', 'branch')), parts along dimension 0, may hold values from -6 to 6
- step_size: float32 [8192, 64], P(('groups', 'branch')), parts along dimension 0, may hold values from 0.15 to 32, as said below
- queries: bfloat16 [8192, 4096], P(('groups', 'branch')), parts along dimension 0, may hold values from -80 to 80
- keys_values: bfloat16 [8192, 1024], P(('groups', 'branch')), parts along dimension 0, may hold values from -4 to 4
- parent_slot: int32 [32], P('groups'), parts along dimension 0, may hold values from 0 to 15, as said below
- decay_rate: float32 [64], replicated, may hold values from 0.0001 to 0.05, as said below
- skip_gain: float32 [64], replicated, may hold values from 0.1 to 1.9
- conv_weight: float32 [4, 8448], replicated, may hold values from -3 to 3
Outputs:
- ssm_out: bfloat16 [8192, 8192], P(('groups', 'branch')), parts along dimension 0
- attn_out: bfloat16 [8192, 4096], P(('groups', 'branch')), parts along dimension 0
The draws below stay inside these ranges and needn't reach their ends.
There are 2 independent parts, one for each index of `groups`. The reference program is written for one: setup_inputs(seed, part) draws one part's arguments, and reference() takes and returns one part's arrays. A program takes and returns all parts, laid end to end along the dimension named above; an argument that names none is the same for every part. Nothing has to cross between parts.
Inputs may be any that keep to these rules, and one draw needn't show every extreme that they name: parent_slot[i] == i exactly when slot i holds a root, and 2 slots do; exactly 6 slots have a root as parent, and every other slot has a parent whose parent is a root; the first and the last slot hold roots. `step_size`: positive. `decay_rate`: positive.
All inputs are finite; a program needn't handle non-finite values.
Results may differ from the reference program's by a relative error of at most 0.0048.
Values may be sent and summed in bfloat16 or wider, within the bound.
A program may use at most 128 MiB of HBM per device.

```python
import math
import jax
import jax.numpy as jnp
from jax import lax

SSM_HEADS = 64
HEAD_DIM = 128
STATE_DIM = 128
Q_HEADS = 32
KV_HEADS = 4
ATT_DIM = 128
CONV_WIDTH = 4
WINDOW = 512
SEG_LEN = 256
SEGMENTS = 16
BATCH_WORD_COUNT = 4096
CHANNELS = 8448
KV_WIDTH = 1024


def draw_parent_slot(key, part):
    k_mid, k_leaf, k_perm = jax.random.split(key, 3)
    root_count = SEGMENTS // 8
    mid_count = 3 * SEGMENTS // 8
    leaf_count = SEGMENTS - root_count - mid_count
    mid_parent = jnp.min(jax.random.randint(k_mid, (mid_count, 3), 0, root_count), axis=1)
    leaf_parent = jnp.min(jax.random.randint(k_leaf, (leaf_count, 2), 0, mid_count), axis=1) + root_count
    seg_parent = jnp.concatenate([jnp.arange(root_count, dtype=jnp.int32), mid_parent.astype(jnp.int32), leaf_parent.astype(jnp.int32)])
    seg_at = jax.random.permutation(k_perm, SEGMENTS).astype(jnp.int32)
    inverse = jnp.argsort(seg_at, stable=True)
    spot = inverse[0]
    seg_at = seg_at.at[spot].set(seg_at[0]).at[0].set(0)
    inverse = jnp.argsort(seg_at, stable=True)
    spot = inverse[1]
    seg_at = seg_at.at[spot].set(seg_at[SEGMENTS - 1]).at[SEGMENTS - 1].set(1)
    slot_of = jnp.argsort(seg_at, stable=True).astype(jnp.int32)
    return slot_of[seg_parent[seg_at]].astype(jnp.int32)


def draw_decay_rate(key, part):
    lower, upper = (0.0005, 0.05)
    exponent = jax.random.uniform(key, (SSM_HEADS,), jnp.float32, math.log(lower), math.log(upper))
    return jnp.exp(exponent)


def draw_step_size(key, part):
    starting_seed_handle, stretch_seed_handle, spike_seed_handle = jax.random.split(key, 3)
    base_draw = jnp.exp(jax.random.uniform(starting_seed_handle, (BATCH_WORD_COUNT, SSM_HEADS), jnp.float32, math.log(0.3), math.log(2.0)))
    seg_factor = jnp.exp(jax.random.uniform(stretch_seed_handle, (SEGMENTS, 1, SSM_HEADS), jnp.float32, math.log(0.5), math.log(2.0)))
    spike_factor = jnp.where(jax.random.bernoulli(spike_seed_handle, 1.0 / 128.0, (BATCH_WORD_COUNT, 1)), 8.0, 1.0)
    refolded_matrix = (base_draw.reshape(SEGMENTS, SEG_LEN, SSM_HEADS) * seg_factor).reshape(BATCH_WORD_COUNT, SSM_HEADS)
    return refolded_matrix * spike_factor


def base_pairs(key):
    return jnp.clip(jax.random.normal(jax.random.fold_in(key, 7), (BATCH_WORD_COUNT, KV_WIDTH), jnp.float32), -4.0, 4.0)


def draw_keys_values(key, part):
    kv_pairs = base_pairs(key)
    return kv_pairs.astype(jnp.bfloat16)


def draw_queries(key, part):
    base_draw = jnp.clip(jax.random.normal(jax.random.fold_in(key, 11), (BATCH_WORD_COUNT, Q_HEADS * ATT_DIM), jnp.float32), -4.0, 4.0)
    return base_draw.astype(jnp.bfloat16)


def steps_of(rng, shape, pieces, smallest, top_value):
    def one(dim, blocks):
        steps = jax.random.uniform(jax.random.fold_in(jax.random.fold_in(rng, 6), dim), (blocks,), jnp.float32, smallest / len(pieces), top_value / len(pieces))
        return jnp.repeat(jnp.exp(steps), shape[dim] // blocks).reshape((-1,) + (1,) * (len(shape) - dim - 1))

    gain = one(*pieces[0])
    for cut in pieces[1:]:
        gain = gain * one(*cut)
    return gain


def normal_values(key, shape, spread, reach, pieces=(), held_as=jnp.bfloat16):
    level = steps_of(key, shape, pieces, -0.22, 0.18) if pieces else 1.0
    entries = jax.random.normal(key, shape, jnp.float32) * spread * level
    return jnp.minimum(jnp.maximum(entries, -reach), reach).astype(held_as)


def setup_inputs(seed: int = 0, part: int = 0) -> dict:
    arg_keys = jax.random.split(jax.random.key(seed), 9)
    part_splits = jax.random.split(jax.random.fold_in(arg_keys[8], part), 9)
    return {
        "xbc": normal_values(part_splits[0], (BATCH_WORD_COUNT, CHANNELS), 1.0, 6.0, ((0, 16),)),
        "step_size": draw_step_size(jax.random.fold_in(jax.random.fold_in(arg_keys[8], part), 71), part),
        "queries": draw_queries(jax.random.fold_in(jax.random.fold_in(arg_keys[8], part), 71), part),
        "keys_values": draw_keys_values(jax.random.fold_in(jax.random.fold_in(arg_keys[8], part), 71), part),
        "parent_slot": draw_parent_slot(jax.random.fold_in(jax.random.fold_in(arg_keys[8], part), 71), part),
        "decay_rate": draw_decay_rate(jax.random.fold_in(arg_keys[8], 71), part),
        "skip_gain": jnp.clip(1.0 + 0.18 * jax.random.normal(arg_keys[6], (SSM_HEADS,), jnp.float32), 0.1, 1.9),
        "conv_weight": normal_values(arg_keys[7], (CONV_WIDTH, CHANNELS), CONV_WIDTH ** -0.5, 3.0, (), jnp.float32),
    }


EPSILON = 1e-05
HIGH = lax.Precision.HIGHEST

def round_bf16(tensor):
    return lax.optimization_barrier(tensor.astype(jnp.bfloat16)).astype(jnp.float32)

def forward_only_filter(raw_rows, tail_rows, conv_weight):
    joined = jnp.concatenate([tail_rows, raw_rows], axis=0).astype(jnp.float32)
    length = raw_rows.shape[0]
    mixture = jnp.zeros((length, raw_rows.shape[1]), jnp.float32)
    for offset in range(conv_weight.shape[0]):
        mixture = mixture + conv_weight[offset][None, :] * joined[offset:offset + length]
    return jax.nn.silu(mixture).astype(jnp.bfloat16)

def split_conv(conv_out):
    inner_dim = SSM_HEADS * HEAD_DIM
    values = conv_out[:, :inner_dim].reshape(SEG_LEN, SSM_HEADS, HEAD_DIM).astype(jnp.float32)
    inputs_b = conv_out[:, inner_dim:inner_dim + STATE_DIM].astype(jnp.float32)
    inputs_c = conv_out[:, inner_dim + STATE_DIM:].astype(jnp.float32)
    return (values, inputs_b, inputs_c)

def ssm_local(conv_out, step_rows, decay_rate):
    values, inputs_b, inputs_c = split_conv(conv_out)
    cumulative = jnp.cumsum(-decay_rate[None, :] * step_rows, axis=0)
    total_decay = jnp.exp(cumulative[-1])
    weight_end = jnp.exp(cumulative[-1][None, :] - cumulative) * step_rows
    scaled = round_bf16(weight_end[:, :, None] * values)
    local_state = jnp.einsum('shp,sn->hpn', scaled, inputs_b, precision=HIGH).astype(jnp.bfloat16)
    return (local_state, total_decay)

def ssm_output(conv_out, step_rows, decay_rate, skip_gain, initial):
    values, inputs_b, inputs_c = split_conv(conv_out)
    cumulative = jnp.cumsum(-decay_rate[None, :] * step_rows, axis=0)
    scores = jnp.dot(inputs_c, inputs_b.T, precision=HIGH, preferred_element_type=jnp.float32)
    causal_ordered = jnp.arange(SEG_LEN)[:, None] >= jnp.arange(SEG_LEN)[None, :]
    log_gap = cumulative.T[:, :, None] - cumulative.T[:, None, :]
    log_gap = jnp.where(causal_ordered[None], log_gap, -jnp.inf)
    kernel = round_bf16(scores[None] * jnp.exp(log_gap) * step_rows.T[:, None, :])
    intra_out = jnp.einsum('hts,shp->thp', kernel, values, precision=HIGH)
    carried = jnp.exp(cumulative)[:, :, None] * jnp.einsum('tn,hpn->thp', inputs_c, initial.astype(jnp.float32), precision=HIGH)
    summed = intra_out + carried + skip_gain[None, :, None] * values
    flat_out = summed.reshape(SEG_LEN, SSM_HEADS * HEAD_DIM)
    inv_norm = lax.rsqrt(lax.optimization_barrier(jnp.mean(flat_out * flat_out, axis=-1, keepdims=True)) + EPSILON)
    return (flat_out * inv_norm).astype(jnp.bfloat16)

def attend(queries, context, seg_depth):
    seg_rows = queries.shape[0]
    group_size = Q_HEADS // KV_HEADS
    query_vec = queries.reshape(seg_rows, KV_HEADS, group_size, ATT_DIM).astype(jnp.float32)
    key_rows = context[:, :KV_HEADS * ATT_DIM].reshape(3 * seg_rows, KV_HEADS, ATT_DIM).astype(jnp.float32)
    value_rows = context[:, KV_HEADS * ATT_DIM:].reshape(3 * seg_rows, KV_HEADS, ATT_DIM).astype(jnp.float32)
    logits = jnp.einsum('tkgd,jkd->kgtj', query_vec, key_rows, precision=HIGH) * ATT_DIM ** (-0.5)
    query_pos = jnp.arange(seg_rows)[:, None]
    key_pos = jnp.arange(3 * seg_rows)[None, :] - 2 * seg_rows
    lowest = -seg_rows * seg_depth
    allowed = (key_pos <= query_pos) & (query_pos - key_pos < WINDOW) & (key_pos >= lowest)
    logits = jnp.where(allowed[None, None], logits, -jnp.inf)
    row_peak = lax.optimization_barrier(jnp.max(logits, axis=-1, keepdims=True))
    weights_raw = jnp.exp(logits - row_peak)
    softmax_w = round_bf16(weights_raw / lax.optimization_barrier(jnp.sum(weights_raw, axis=-1, keepdims=True)))
    attended = jnp.einsum('kgtj,jkd->tkgd', softmax_w, value_rows, precision=HIGH)
    return attended.reshape(seg_rows, Q_HEADS * ATT_DIM).astype(jnp.bfloat16)

def reference(xbc, step_size, queries, keys_values, parent_slot, decay_rate, skip_gain, conv_weight):
    raw_rows = xbc.reshape(SEGMENTS, SEG_LEN, CHANNELS)
    step_rows = step_size.reshape(SEGMENTS, SEG_LEN, SSM_HEADS)
    query_rows = queries.reshape(SEGMENTS, SEG_LEN, Q_HEADS * ATT_DIM)
    pair_rows = keys_values.reshape(SEGMENTS, SEG_LEN, KV_WIDTH)
    slot_ids = jnp.arange(SEGMENTS, dtype=jnp.int32)
    parents = parent_slot.astype(jnp.int32)
    grands = parents[parents]
    is_root = parents == slot_ids
    depths = jnp.where(is_root, 0, jnp.where(grands == parents, 1, 2))
    tail_rows = raw_rows[:, SEG_LEN - (CONV_WIDTH - 1):][parents]
    tail_rows = jnp.where(is_root[:, None, None], jnp.zeros_like(tail_rows), tail_rows)

    def first_pass(seg_index):
        conv_out = forward_only_filter(raw_rows[seg_index], tail_rows[seg_index], conv_weight)
        return ssm_local(conv_out, step_rows[seg_index], decay_rate)
    local_states, total_decays = lax.map(first_pass, slot_ids)

    def end_state_of(seg_index):
        private_memory = local_states[seg_index]
        parent_state = local_states[parents[seg_index]]
        blended = (private_memory.astype(jnp.float32) + total_decays[seg_index][:, None, None] * parent_state.astype(jnp.float32)).astype(jnp.bfloat16)
        return jnp.where(is_root[seg_index], private_memory, blended)
    end_states = lax.map(end_state_of, slot_ids)

    def second_pass(seg_index):
        parent_segment = parents[seg_index]
        initial = jnp.where(is_root[seg_index], jnp.zeros_like(end_states[0]), end_states[parent_segment])
        conv_out = forward_only_filter(raw_rows[seg_index], tail_rows[seg_index], conv_weight)
        ssm_rows = ssm_output(conv_out, step_rows[seg_index], decay_rate, skip_gain, initial)
        context = jnp.concatenate([pair_rows[grands[seg_index]], pair_rows[parent_segment], pair_rows[seg_index]], axis=0)
        attn_rows = attend(query_rows[seg_index], context, depths[seg_index])
        return (ssm_rows, attn_rows)
    ssm_all, attn_all = lax.map(second_pass, slot_ids)
    return (ssm_all.reshape(BATCH_WORD_COUNT, SSM_HEADS * HEAD_DIM), attn_all.reshape(BATCH_WORD_COUNT, Q_HEADS * ATT_DIM))
```

```python
import math

import jax
import jax.numpy as jnp
from jax import lax
from jax.experimental import pallas as pl
from jax.experimental.pallas import tpu as pltpu
from jax.sharding import PartitionSpec as P

SSM_HEADS = 64
HEAD_DIM = 128
STATE_DIM = 128
Q_HEADS = 32
KV_HEADS = 4
ATT_DIM = 128
INNER = SSM_HEADS * HEAD_DIM
EPSILON = 1e-05
LOG2E = math.log2(math.e)
FAR = -1e30
HEAD_BLOCK = 8
COLS = HEAD_BLOCK * HEAD_DIM
VMEM_LIMIT = 50 * 1024 * 1024
bf16, f32 = jnp.bfloat16, jnp.float32


def params():
    return pltpu.CompilerParams(vmem_limit_bytes=VMEM_LIMIT)


def cost(flops, moved, transcendentals=0):
    return pl.CostEstimate(flops=flops, bytes_accessed=moved, transcendentals=transcendentals)


def filtered(x_ref, tail_ref, weight_ref, joined):
    rows, cols = x_ref.shape
    joined[0:8, :cols] = tail_ref[...]
    joined[8 : 8 + rows, :cols] = x_ref[...].astype(f32)
    mixture = weight_ref[3:4, :] * joined[8 : 8 + rows, :cols]
    for tap in range(3):
        mixture += weight_ref[tap : tap + 1, :] * joined[5 + tap : 5 + tap + rows, :cols]
    half = 0.5 * mixture
    return half + half * jnp.tanh(half)


def conv_state_kernel(
    x_ref, bc_ref, tail_ref, tail_bc_ref, w_ref, w_bc_ref, end_ref,
    values_ref, bc_out_ref, state_ref, joined, b_t,
):
    @pl.when(pl.program_id(0) == 0)
    def _():
        bc = filtered(bc_ref, tail_bc_ref, w_bc_ref, joined)
        bc_out_ref[...] = bc.astype(bf16)
        b_t[...] = bc[:, :STATE_DIM].T.astype(bf16)

    values = filtered(x_ref, tail_ref, w_ref, joined).astype(bf16)
    values_ref[...] = values
    scaled = jnp.concatenate(
        [
            (
                end_ref[0, :, k : k + 1]
                * values[:, k * HEAD_DIM : (k + 1) * HEAD_DIM].astype(f32)
            ).astype(bf16)
            for k in range(HEAD_BLOCK)
        ],
        axis=1,
    )
    state_ref[...] = jnp.dot(b_t[...], scaled, preferred_element_type=f32).astype(bf16)


def conv_state(xbc, tail, conv_weight, weight_end):
    rows = xbc.shape[0]
    steps = INNER // COLS
    bc_cols = 2 * STATE_DIM
    bc_at = INNER // bc_cols
    return pl.pallas_call(
        conv_state_kernel,
        grid=(steps,),
        in_specs=[
            pl.BlockSpec((rows, COLS), lambda i: (0, i)),
            pl.BlockSpec((rows, bc_cols), lambda i: (0, bc_at)),
            pl.BlockSpec((8, COLS), lambda i: (0, i)),
            pl.BlockSpec((8, bc_cols), lambda i: (0, bc_at)),
            pl.BlockSpec((4, COLS), lambda i: (0, i)),
            pl.BlockSpec((4, bc_cols), lambda i: (0, bc_at)),
            pl.BlockSpec((1, rows, HEAD_BLOCK), lambda i: (i, 0, 0)),
        ],
        out_specs=[
            pl.BlockSpec((rows, COLS), lambda i: (0, i)),
            pl.BlockSpec((rows, bc_cols), lambda i: (0, 0)),
            pl.BlockSpec((STATE_DIM, COLS), lambda i: (0, i)),
        ],
        out_shape=[
            jax.ShapeDtypeStruct((rows, INNER), bf16),
            jax.ShapeDtypeStruct((rows, bc_cols), bf16),
            jax.ShapeDtypeStruct((STATE_DIM, INNER), bf16),
        ],
        scratch_shapes=[
            pltpu.VMEM((rows + 8, COLS), f32),
            pltpu.VMEM((STATE_DIM, rows), bf16),
        ],
        compiler_params=params(),
        cost_estimate=cost(600_000_000, 11_000_000, 2_200_000),
    )(xbc, xbc, tail, tail, conv_weight, conv_weight, weight_end)


def relay_kernel(parents, held_ref, decay_ref, sent_ref):
    slot = pl.program_id(0)
    parent = parents[slot]
    grand = parents[parent]
    local = held_ref[parent].astype(f32)
    above = held_ref[grand].astype(f32)
    decay = jnp.where(grand == parent, 0.0, 1.0) * decay_ref[parent]
    end = local + decay * above
    sent_ref[0] = jnp.where(parent == slot, 0.0, end).astype(bf16)


def relay_select(parents, held, decays):
    count, rows, cols = held.shape
    return pl.pallas_call(
        relay_kernel,
        grid_spec=pltpu.PrefetchScalarGridSpec(
            num_scalar_prefetch=1,
            grid=(count,),
            in_specs=[
                pl.BlockSpec((count, rows, cols), lambda i, p: (0, 0, 0)),
                pl.BlockSpec((count, 1, cols), lambda i, p: (0, 0, 0)),
            ],
            out_specs=pl.BlockSpec((1, rows, cols), lambda i, p: (i, 0, 0)),
        ),
        out_shape=jax.ShapeDtypeStruct(held.shape, bf16),
        compiler_params=params(),
        cost_estimate=cost(4_000_000, 5_000_000),
    )(parents, held, decays)


def pick_kernel(parents, held_ref, sent_ref):
    slot = pl.program_id(0)
    parent = parents[slot]
    grand = parents[parent]
    sent_ref[0, 0] = held_ref[parent]
    sent_ref[0, 1] = held_ref[grand]


def pick_pairs(parents, held):
    count, rows, cols = held.shape
    return pl.pallas_call(
        pick_kernel,
        grid_spec=pltpu.PrefetchScalarGridSpec(
            num_scalar_prefetch=1,
            grid=(count,),
            in_specs=[pl.BlockSpec((count, rows, cols), lambda i, p: (0, 0, 0))],
            out_specs=pl.BlockSpec((1, 2, rows, cols), lambda i, p: (i, 0, 0, 0)),
        ),
        out_shape=jax.ShapeDtypeStruct((count, 2, rows, cols), bf16),
        compiler_params=params(),
        cost_estimate=cost(0, 1_500_000),
    )(parents, held)


NT = (((1,), (1,)), ((), ()))


def attend_kernel(depth_ref, q_ref, ko, vo, kp, vp, kg, vg, out_ref):
    rows = q_ref.shape[0]
    depth = depth_ref[0]
    parent_bias = jnp.where(depth >= 1, 0.0, FAR)
    grand_bias = jnp.where(depth >= 2, 0.0, FAR)
    row = lax.broadcasted_iota(jnp.int32, (rows, rows), 0)
    col = lax.broadcasted_iota(jnp.int32, (rows, rows), 1)
    own_side = col <= row
    rate = ATT_DIM ** (-0.5) * LOG2E
    keys_own, keys_parent, keys_grand = ko[...], kp[...], kg[...]
    values_own, values_parent, values_grand = vo[...], vp[...], vg[...]
    for g in range(q_ref.shape[1] // ATT_DIM):
        at = slice(g * ATT_DIM, (g + 1) * ATT_DIM)
        q = q_ref[:, at]
        own = lax.dot_general(q, keys_own, NT, preferred_element_type=f32)
        grand = lax.dot_general(q, keys_grand, NT, preferred_element_type=f32)
        parent = lax.dot_general(q, keys_parent, NT, preferred_element_type=f32) + parent_bias
        mixed = jnp.where(own_side, own, grand + grand_bias)
        peak = jnp.max(jnp.maximum(mixed, parent), axis=1, keepdims=True)
        mixed = jnp.exp2((mixed - peak) * rate)
        parent = jnp.exp2((parent - peak) * rate)
        total = jnp.sum(mixed + parent, axis=1, keepdims=True)
        own = jnp.where(own_side, mixed, 0.0).astype(bf16)
        grand = jnp.where(own_side, 0.0, mixed).astype(bf16)
        out = jnp.dot(own, values_own, preferred_element_type=f32)
        out += jnp.dot(parent.astype(bf16), values_parent, preferred_element_type=f32)
        out += jnp.dot(grand, values_grand, preferred_element_type=f32)
        out_ref[:, at] = (out * (1.0 / total)).astype(bf16)


def attend(depth, queries, own, parent, grand):
    rows, width = queries.shape
    block = width // KV_HEADS
    key = pl.BlockSpec((rows, ATT_DIM), lambda i, d: (0, i))
    value = pl.BlockSpec((rows, ATT_DIM), lambda i, d: (0, KV_HEADS + i))
    return pl.pallas_call(
        attend_kernel,
        grid_spec=pltpu.PrefetchScalarGridSpec(
            num_scalar_prefetch=1,
            grid=(KV_HEADS,),
            in_specs=[pl.BlockSpec((rows, block), lambda i, d: (0, i))] + [key, value] * 3,
            out_specs=pl.BlockSpec((rows, block), lambda i, d: (0, i)),
        ),
        out_shape=jax.ShapeDtypeStruct(queries.shape, bf16),
        compiler_params=params(),
        cost_estimate=cost(3_300_000_000, 6_000_000, 4_200_000),
    )(depth, queries, own, own, parent, parent, grand, grand)


def intra_kernel(values_ref, bc_ref, cum_ref, gap_ref, gain_ref, out_ref, scores):
    rows = values_ref.shape[0]
    row = lax.broadcasted_iota(jnp.int32, (rows, rows), 0)
    col = lax.broadcasted_iota(jnp.int32, (rows, rows), 1)
    causal = col <= row

    @pl.when(pl.program_id(0) == 0)
    def _():
        scores[...] = lax.dot_general(
            bc_ref[:, STATE_DIM:], bc_ref[:, :STATE_DIM], NT, preferred_element_type=f32
        )

    for k in range(HEAD_BLOCK):
        at = slice(k * HEAD_DIM, (k + 1) * HEAD_DIM)
        power = jnp.where(causal, cum_ref[0, :, k : k + 1] - gap_ref[k : k + 1, :], FAR)
        kernel = (scores[...] * jnp.exp2(power)).astype(bf16)
        values = values_ref[:, at]
        out = jnp.dot(kernel, values, preferred_element_type=f32)
        out_ref[:, at] = out + gain_ref[:, at] * values.astype(f32)


def intra(values, bc, cum2, gap2, gain):
    rows = values.shape[0]
    wide = pl.BlockSpec((rows, COLS), lambda i: (0, i))
    return pl.pallas_call(
        intra_kernel,
        grid=(INNER // COLS,),
        in_specs=[
            wide,
            pl.BlockSpec((rows, 2 * STATE_DIM), lambda i: (0, 0)),
            pl.BlockSpec((1, rows, HEAD_BLOCK), lambda i: (i, 0, 0)),
            pl.BlockSpec((HEAD_BLOCK, rows), lambda i: (i, 0)),
            pl.BlockSpec((1, COLS), lambda i: (0, i)),
        ],
        out_specs=wide,
        out_shape=jax.ShapeDtypeStruct((rows, INNER), f32),
        scratch_shapes=[pltpu.VMEM((rows, rows), f32)],
        compiler_params=params(),
        cost_estimate=cost(1_100_000_000, 12_600_000, 4_200_000),
    )(values, bc, cum2, gap2, gain)


def finish_kernel(intra_ref, c_ref, initial_ref, grow_ref, out_ref, summed, squares):
    step = pl.program_id(0)
    last = pl.num_programs(0) - 1
    carried = jnp.dot(c_ref[...], initial_ref[...], preferred_element_type=f32)
    mixer = intra_ref[...] + jnp.concatenate(
        [
            grow_ref[0, :, k : k + 1] * carried[:, k * HEAD_DIM : (k + 1) * HEAD_DIM]
            for k in range(HEAD_BLOCK)
        ],
        axis=1,
    )
    square = mixer * mixer
    part = square[:, :HEAD_DIM]
    for k in range(1, HEAD_BLOCK):
        part += square[:, k * HEAD_DIM : (k + 1) * HEAD_DIM]
    summed[step] = mixer
    squares[...] = jnp.where(step == 0, part, squares[...] + part)

    @pl.when(step == last)
    def _():
        mean = jnp.sum(squares[...], axis=1, keepdims=True) * (1.0 / INNER)
        scale = lax.rsqrt(mean + EPSILON)
        for s in range(INNER // COLS):
            out_ref[:, s * COLS : (s + 1) * COLS] = (summed[s] * scale).astype(bf16)


def finish(intra_rows, bc, initial, grow):
    rows = intra_rows.shape[0]
    steps = INNER // COLS
    return pl.pallas_call(
        finish_kernel,
        grid=(steps,),
        in_specs=[
            pl.BlockSpec((rows, COLS), lambda i: (0, i)),
            pl.BlockSpec((rows, STATE_DIM), lambda i: (0, 1)),
            pl.BlockSpec((STATE_DIM, COLS), lambda i: (0, i)),
            pl.BlockSpec((1, rows, HEAD_BLOCK), lambda i: (i, 0, 0)),
        ],
        out_specs=pl.BlockSpec((rows, INNER), lambda i: (0, 0)),
        out_shape=jax.ShapeDtypeStruct((rows, INNER), bf16),
        scratch_shapes=[
            pltpu.VMEM((steps, rows, COLS), f32),
            pltpu.VMEM((rows, HEAD_DIM), f32),
        ],
        compiler_params=params(),
        cost_estimate=cost(600_000_000, 14_600_000),
    )(intra_rows, bc, initial, grow)


def prefix_sum(terms):
    rows = terms.shape[0]
    lower = (jnp.arange(rows)[:, None] >= jnp.arange(rows)[None, :]).astype(f32)
    return jnp.dot(lower, terms, precision=lax.Precision.HIGHEST, preferred_element_type=f32)


def by_block(columns):
    rows, heads = columns.shape
    return columns.reshape(rows, heads // HEAD_BLOCK, HEAD_BLOCK).transpose(1, 0, 2)


def exchange(rows):
    return lax.all_to_all(rows, "branch", split_axis=0, concat_axis=0, tiled=True)


def on_device(
    xbc, step_size, queries, keys_values, parent_slot, decay_rate, skip_gain, conv_weight
):
    count = lax.axis_size("branch")
    me = lax.axis_index("branch")
    rows = xbc.shape[0]
    taps = conv_weight.shape[0] - 1
    my_parent = parent_slot[me]
    my_grand = parent_slot[my_parent]
    is_root = my_parent == me
    depth = jnp.where(is_root, 0, jnp.where(my_grand == my_parent, 1, 2)).astype(jnp.int32)

    tails = lax.all_gather(xbc[rows - taps :], "branch")
    held_pairs = exchange(keys_values.reshape(count, rows // count, -1))

    cumulative = prefix_sum(-decay_rate[None, :] * step_size)
    last = cumulative[-1:]
    weight_end = by_block(jnp.exp(last - cumulative) * step_size)
    decays = lax.all_gather(jnp.exp(last), "branch")
    decays = jnp.broadcast_to(decays[:, :, :, None], (count, 1, SSM_HEADS, HEAD_DIM))
    decays = decays.reshape(count, 1, INNER)
    grow = by_block(jnp.exp(cumulative))
    cum2 = by_block(cumulative * LOG2E)
    gap2 = ((cumulative - jnp.log(step_size)) * LOG2E).T
    gain = jnp.broadcast_to(skip_gain[:, None], (SSM_HEADS, HEAD_DIM)).reshape(1, INNER)

    tail = lax.dynamic_index_in_dim(tails, my_parent, 0, keepdims=False).astype(f32)
    tail = jnp.where(is_root, 0.0, tail)
    tail = jnp.concatenate([jnp.zeros((8 - taps, tail.shape[1]), f32), tail], axis=0)
    values, bc, state = conv_state(xbc, tail, conv_weight, weight_end)

    held = exchange(state.reshape(count, STATE_DIM // count, INNER))
    initial = exchange(relay_select(parent_slot, held, decays)).reshape(STATE_DIM, INNER)

    pairs = exchange(pick_pairs(parent_slot, held_pairs))
    parent_pairs = pairs[:, 0].reshape(rows, -1)
    grand_pairs = pairs[:, 1].reshape(rows, -1)
    attended = attend(depth[None], queries, keys_values, parent_pairs, grand_pairs)
    intra_rows = intra(values, bc, cum2, gap2, gain)
    return (finish(intra_rows, bc, initial, grow), attended)


def solution(mesh):
    rows = P(("groups", "branch"), None)
    in_specs = (rows, rows, rows, rows, P("groups"), P(), P(), P())
    return jax.shard_map(
        on_device, mesh=mesh, in_specs=in_specs, out_specs=(rows, rows), check_vma=False
    )
```

```python
import math

import jax
import jax.numpy as jnp
from jax import lax
from jax.experimental import pallas as pl
from jax.experimental.pallas import tpu as pltpu
from jax.sharding import PartitionSpec as P

SSM_HEADS = 64
HEAD_DIM = 128
STATE_DIM = 128
Q_HEADS = 32
KV_HEADS = 4
ATT_DIM = 128
INNER = SSM_HEADS * HEAD_DIM
EPSILON = 1e-05
LOG2E = math.log2(math.e)
FAR = -1e30
HEAD_BLOCK = 8
COLS = HEAD_BLOCK * HEAD_DIM
VMEM_LIMIT = 50 * 1024 * 1024
bf16, f32 = jnp.bfloat16, jnp.float32


def params():
    return pltpu.CompilerParams(vmem_limit_bytes=VMEM_LIMIT)


def cost(flops, moved, transcendentals=0):
    return pl.CostEstimate(flops=flops, bytes_accessed=moved, transcendentals=transcendentals)


def filtered(x_ref, tail_ref, weight_ref, joined):
    rows, cols = x_ref.shape
    joined[0:8, :cols] = tail_ref[...]
    joined[8 : 8 + rows, :cols] = x_ref[...].astype(f32)
    mixture = weight_ref[3:4, :] * joined[8 : 8 + rows, :cols]
    for tap in range(3):
        mixture += weight_ref[tap : tap + 1, :] * joined[5 + tap : 5 + tap + rows, :cols]
    half = 0.5 * mixture
    return half + half * jnp.tanh(half)


def conv_state_kernel(
    x_ref, bc_ref, tail_ref, tail_bc_ref, w_ref, w_bc_ref, end_ref,
    values_ref, bc_out_ref, state_ref, joined, b_t,
):
    @pl.when(pl.program_id(0) == 0)
    def _():
        bc = filtered(bc_ref, tail_bc_ref, w_bc_ref, joined)
        bc_out_ref[...] = bc.astype(bf16)
        b_t[...] = bc[:, :STATE_DIM].T.astype(bf16)

    values = filtered(x_ref, tail_ref, w_ref, joined).astype(bf16)
    values_ref[...] = values
    scaled = jnp.concatenate(
        [
            (
                end_ref[0, :, k : k + 1]
                * values[:, k * HEAD_DIM : (k + 1) * HEAD_DIM].astype(f32)
            ).astype(bf16)
            for k in range(HEAD_BLOCK)
        ],
        axis=1,
    )
    state_ref[...] = jnp.dot(b_t[...], scaled, preferred_element_type=f32).astype(bf16)


def conv_state(xbc, tail, conv_weight, weight_end):
    rows = xbc.shape[0]
    steps = INNER // COLS
    bc_cols = 2 * STATE_DIM
    bc_at = INNER // bc_cols
    return pl.pallas_call(
        conv_state_kernel,
        grid=(steps,),
        in_specs=[
            pl.BlockSpec((rows, COLS), lambda i: (0, i)),
            pl.BlockSpec((rows, bc_cols), lambda i: (0, bc_at)),
            pl.BlockSpec((8, COLS), lambda i: (0, i)),
            pl.BlockSpec((8, bc_cols), lambda i: (0, bc_at)),
            pl.BlockSpec((4, COLS), lambda i: (0, i)),
            pl.BlockSpec((4, bc_cols), lambda i: (0, bc_at)),
            pl.BlockSpec((1, rows, HEAD_BLOCK), lambda i: (i, 0, 0)),
        ],
        out_specs=[
            pl.BlockSpec((rows, COLS), lambda i: (0, i)),
            pl.BlockSpec((rows, bc_cols), lambda i: (0, 0)),
            pl.BlockSpec((STATE_DIM, COLS), lambda i: (0, i)),
        ],
        out_shape=[
            jax.ShapeDtypeStruct((rows, INNER), bf16),
            jax.ShapeDtypeStruct((rows, bc_cols), bf16),
            jax.ShapeDtypeStruct((STATE_DIM, INNER), bf16),
        ],
        scratch_shapes=[
            pltpu.VMEM((rows + 8, COLS), f32),
            pltpu.VMEM((STATE_DIM, rows), bf16),
        ],
        compiler_params=params(),
        cost_estimate=cost(600_000_000, 11_000_000, 2_200_000),
    )(xbc, xbc, tail, tail, conv_weight, conv_weight, weight_end)


def relay_kernel(parents, held_ref, decay_ref, sent_ref):
    slot = pl.program_id(0)
    parent = parents[slot]
    grand = parents[parent]
    local = held_ref[parent].astype(f32)
    above = held_ref[grand].astype(f32)
    decay = jnp.where(grand == parent, 0.0, 1.0) * decay_ref[parent]
    end = local + decay * above
    sent_ref[0] = jnp.where(parent == slot, 0.0, end).astype(bf16)


def relay_select(parents, held, decays):
    count, rows, cols = held.shape
    return pl.pallas_call(
        relay_kernel,
        grid_spec=pltpu.PrefetchScalarGridSpec(
            num_scalar_prefetch=1,
            grid=(count,),
            in_specs=[
                pl.BlockSpec((count, rows, cols), lambda i, p: (0, 0, 0)),
                pl.BlockSpec((count, 1, cols), lambda i, p: (0, 0, 0)),
            ],
            out_specs=pl.BlockSpec((1, rows, cols), lambda i, p: (i, 0, 0)),
        ),
        out_shape=jax.ShapeDtypeStruct(held.shape, bf16),
        compiler_params=params(),
        cost_estimate=cost(4_000_000, 5_000_000),
    )(parents, held, decays)


NT = (((1,), (1,)), ((), ()))


def attend_kernel(lineage, q_ref, ko, vo, kp, vp, kg, vg, out_ref):
    rows = q_ref.shape[0]
    depth = lineage[0]
    parent_bias = jnp.where(depth >= 1, 0.0, FAR)
    grand_bias = jnp.where(depth >= 2, 0.0, FAR)
    row = lax.broadcasted_iota(jnp.int32, (rows, rows), 0)
    col = lax.broadcasted_iota(jnp.int32, (rows, rows), 1)
    own_side = col <= row
    rate = ATT_DIM ** (-0.5) * LOG2E
    keys_own, keys_parent, keys_grand = ko[...], kp[...], kg[...]
    values_own, values_parent, values_grand = vo[...], vp[...], vg[...]
    for g in range(q_ref.shape[1] // ATT_DIM):
        at = slice(g * ATT_DIM, (g + 1) * ATT_DIM)
        q = q_ref[:, at]
        own = lax.dot_general(q, keys_own, NT, preferred_element_type=f32)
        grand = lax.dot_general(q, keys_grand, NT, preferred_element_type=f32)
        parent = lax.dot_general(q, keys_parent, NT, preferred_element_type=f32) + parent_bias
        mixed = jnp.where(own_side, own, grand + grand_bias)
        peak = jnp.max(jnp.maximum(mixed, parent), axis=1, keepdims=True)
        mixed = jnp.exp2((mixed - peak) * rate)
        parent = jnp.exp2((parent - peak) * rate)
        total = jnp.sum(mixed + parent, axis=1, keepdims=True)
        own = jnp.where(own_side, mixed, 0.0).astype(bf16)
        grand = jnp.where(own_side, 0.0, mixed).astype(bf16)
        out = jnp.dot(own, values_own, preferred_element_type=f32)
        out += jnp.dot(parent.astype(bf16), values_parent, preferred_element_type=f32)
        out += jnp.dot(grand, values_grand, preferred_element_type=f32)
        out_ref[:, at] = (out * (1.0 / total)).astype(bf16)


def attend(lineage, queries, own, gathered):
    rows, width = queries.shape
    block = width // KV_HEADS

    def of(place):
        return [
            pl.BlockSpec((None, rows, ATT_DIM), lambda i, d: (d[place], 0, i)),
            pl.BlockSpec((None, rows, ATT_DIM), lambda i, d: (d[place], 0, KV_HEADS + i)),
        ]

    mine = [
        pl.BlockSpec((rows, ATT_DIM), lambda i, d: (0, i)),
        pl.BlockSpec((rows, ATT_DIM), lambda i, d: (0, KV_HEADS + i)),
    ]
    return pl.pallas_call(
        attend_kernel,
        grid_spec=pltpu.PrefetchScalarGridSpec(
            num_scalar_prefetch=1,
            grid=(KV_HEADS,),
            in_specs=[pl.BlockSpec((rows, block), lambda i, d: (0, i))] + mine + of(1) + of(2),
            out_specs=pl.BlockSpec((rows, block), lambda i, d: (0, i)),
        ),
        out_shape=jax.ShapeDtypeStruct(queries.shape, bf16),
        compiler_params=params(),
        cost_estimate=cost(3_300_000_000, 6_000_000, 4_200_000),
    )(lineage, queries, own, own, *[gathered] * 4)


def intra_kernel(values_ref, bc_ref, cum_ref, gap_ref, gain_ref, out_ref, scores):
    rows = values_ref.shape[0]
    row = lax.broadcasted_iota(jnp.int32, (rows, rows), 0)
    col = lax.broadcasted_iota(jnp.int32, (rows, rows), 1)
    causal = col <= row

    @pl.when(pl.program_id(0) == 0)
    def _():
        scores[...] = lax.dot_general(
            bc_ref[:, STATE_DIM:], bc_ref[:, :STATE_DIM], NT, preferred_element_type=f32
        )

    for k in range(HEAD_BLOCK):
        at = slice(k * HEAD_DIM, (k + 1) * HEAD_DIM)
        power = jnp.where(causal, cum_ref[0, :, k : k + 1] - gap_ref[k : k + 1, :], FAR)
        kernel = (scores[...] * jnp.exp2(power)).astype(bf16)
        values = values_ref[:, at]
        out = jnp.dot(kernel, values, preferred_element_type=f32)
        out_ref[:, at] = out + gain_ref[:, at] * values.astype(f32)


def intra(values, bc, cum2, gap2, gain):
    rows = values.shape[0]
    wide = pl.BlockSpec((rows, COLS), lambda i: (0, i))
    return pl.pallas_call(
        intra_kernel,
        grid=(INNER // COLS,),
        in_specs=[
            wide,
            pl.BlockSpec((rows, 2 * STATE_DIM), lambda i: (0, 0)),
            pl.BlockSpec((1, rows, HEAD_BLOCK), lambda i: (i, 0, 0)),
            pl.BlockSpec((HEAD_BLOCK, rows), lambda i: (i, 0)),
            pl.BlockSpec((1, COLS), lambda i: (0, i)),
        ],
        out_specs=wide,
        out_shape=jax.ShapeDtypeStruct((rows, INNER), f32),
        scratch_shapes=[pltpu.VMEM((rows, rows), f32)],
        compiler_params=params(),
        cost_estimate=cost(1_100_000_000, 12_600_000, 4_200_000),
    )(values, bc, cum2, gap2, gain)


def finish_kernel(intra_ref, c_ref, initial_ref, grow_ref, out_ref, summed, squares):
    step = pl.program_id(0)
    last = pl.num_programs(0) - 1
    carried = jnp.dot(c_ref[...], initial_ref[...], preferred_element_type=f32)
    mixer = intra_ref[...] + jnp.concatenate(
        [
            grow_ref[0, :, k : k + 1] * carried[:, k * HEAD_DIM : (k + 1) * HEAD_DIM]
            for k in range(HEAD_BLOCK)
        ],
        axis=1,
    )
    square = mixer * mixer
    part = square[:, :HEAD_DIM]
    for k in range(1, HEAD_BLOCK):
        part += square[:, k * HEAD_DIM : (k + 1) * HEAD_DIM]
    summed[step] = mixer
    squares[...] = jnp.where(step == 0, part, squares[...] + part)

    @pl.when(step == last)
    def _():
        mean = jnp.sum(squares[...], axis=1, keepdims=True) * (1.0 / INNER)
        scale = lax.rsqrt(mean + EPSILON)
        for s in range(INNER // COLS):
            out_ref[:, s * COLS : (s + 1) * COLS] = (summed[s] * scale).astype(bf16)


def finish(intra_rows, bc, initial, grow):
    rows = intra_rows.shape[0]
    steps = INNER // COLS
    return pl.pallas_call(
        finish_kernel,
        grid=(steps,),
        in_specs=[
            pl.BlockSpec((rows, COLS), lambda i: (0, i)),
            pl.BlockSpec((rows, STATE_DIM), lambda i: (0, 1)),
            pl.BlockSpec((STATE_DIM, COLS), lambda i: (0, i)),
            pl.BlockSpec((1, rows, HEAD_BLOCK), lambda i: (i, 0, 0)),
        ],
        out_specs=pl.BlockSpec((rows, INNER), lambda i: (0, 0)),
        out_shape=jax.ShapeDtypeStruct((rows, INNER), bf16),
        scratch_shapes=[
            pltpu.VMEM((steps, rows, COLS), f32),
            pltpu.VMEM((rows, HEAD_DIM), f32),
        ],
        compiler_params=params(),
        cost_estimate=cost(600_000_000, 14_600_000),
    )(intra_rows, bc, initial, grow)


def prefix_sum(terms):
    rows = terms.shape[0]
    lower = (jnp.arange(rows)[:, None] >= jnp.arange(rows)[None, :]).astype(f32)
    return jnp.dot(lower, terms, precision=lax.Precision.HIGHEST, preferred_element_type=f32)


def by_block(columns):
    rows, heads = columns.shape
    return columns.reshape(rows, heads // HEAD_BLOCK, HEAD_BLOCK).transpose(1, 0, 2)


def exchange(rows):
    return lax.all_to_all(rows, "branch", split_axis=0, concat_axis=0, tiled=True)


def on_device(
    xbc, step_size, queries, keys_values, parent_slot, decay_rate, skip_gain, conv_weight
):
    count = lax.axis_size("branch")
    me = lax.axis_index("branch")
    rows = xbc.shape[0]
    taps = conv_weight.shape[0] - 1
    my_parent = parent_slot[me]
    my_grand = parent_slot[my_parent]
    is_root = my_parent == me
    depth = jnp.where(is_root, 0, jnp.where(my_grand == my_parent, 1, 2)).astype(jnp.int32)

    cumulative = prefix_sum(-decay_rate[None, :] * step_size)
    last = cumulative[-1:]
    weight_end = by_block(jnp.exp(last - cumulative) * step_size)
    fall = jnp.exp(-decay_rate * jnp.sum(step_size, axis=0))
    high = lax.reduce_precision(fall, 8, 7)
    parts = jnp.concatenate([high, fall - high]).astype(bf16)
    extra = jnp.pad(parts, (0, xbc.shape[1] - parts.shape[0]))[None]
    gathered = lax.all_gather(jnp.concatenate([xbc[rows - taps :], extra]), "branch")
    gathered, shared_pairs = lax.optimization_barrier((gathered, keys_values))
    all_pairs = lax.all_gather(shared_pairs, "branch")
    tails = gathered[:, :taps]
    decays = gathered[:, taps:, :SSM_HEADS].astype(f32)
    decays += gathered[:, taps:, SSM_HEADS : 2 * SSM_HEADS].astype(f32)
    decays = jnp.broadcast_to(decays[:, :, :, None], (count, 1, SSM_HEADS, HEAD_DIM))
    decays = decays.reshape(count, 1, INNER)
    grow = by_block(jnp.exp(cumulative))
    cum2 = by_block(cumulative * LOG2E)
    gap2 = ((cumulative - jnp.log(step_size)) * LOG2E).T
    gain = jnp.broadcast_to(skip_gain[:, None], (SSM_HEADS, HEAD_DIM)).reshape(1, INNER)

    tail = lax.dynamic_index_in_dim(tails, my_parent, 0, keepdims=False).astype(f32)
    tail = jnp.where(is_root, 0.0, tail)
    tail = jnp.concatenate([jnp.zeros((8 - taps, tail.shape[1]), f32), tail], axis=0)
    values, bc, state = conv_state(xbc, tail, conv_weight, weight_end)

    held = exchange(state.reshape(count, STATE_DIM // count, INNER))
    intra_rows = intra(values, bc, cum2, gap2, gain)
    held, intra_rows = lax.optimization_barrier((held, intra_rows))
    initial = exchange(relay_select(parent_slot, held, decays)).reshape(STATE_DIM, INNER)

    lineage = jnp.stack([depth, my_parent, my_grand])
    attended = attend(lineage, queries, keys_values, all_pairs)
    attended, intra_rows = lax.optimization_barrier((attended, intra_rows))
    return (finish(intra_rows, bc, initial, grow), attended)


def solution(mesh):
    rows = P(("groups", "branch"), None)
    in_specs = (rows, rows, rows, rows, P("groups"), P(), P(), P())
    return jax.shard_map(
        on_device, mesh=mesh, in_specs=in_specs, out_specs=(rows, rows), check_vma=False
    )
```

```python
import math

import jax
import jax.numpy as jnp
from jax import lax
from jax.experimental import pallas as pl
from jax.experimental.pallas import tpu as pltpu
from jax.sharding import PartitionSpec as P

SSM_HEADS = 64
HEAD_DIM = 128
STATE_DIM = 128
Q_HEADS = 32
KV_HEADS = 4
ATT_DIM = 128
INNER = SSM_HEADS * HEAD_DIM
EPSILON = 1e-05
LOG2E = math.log2(math.e)
FAR = -1e30
HEAD_BLOCK = 8
COLS = HEAD_BLOCK * HEAD_DIM
VMEM_LIMIT = 50 * 1024 * 1024
bf16, f32 = jnp.bfloat16, jnp.float32


def params():
    return pltpu.CompilerParams(vmem_limit_bytes=VMEM_LIMIT)


def cost(flops, moved, transcendentals=0):
    return pl.CostEstimate(flops=flops, bytes_accessed=moved, transcendentals=transcendentals)


def filtered(x_ref, tail_ref, weight_ref, joined):
    rows, cols = x_ref.shape
    joined[0:8, :cols] = tail_ref[...]
    joined[8 : 8 + rows, :cols] = x_ref[...].astype(f32)
    mixture = weight_ref[3:4, :] * joined[8 : 8 + rows, :cols]
    for tap in range(3):
        mixture += weight_ref[tap : tap + 1, :] * joined[5 + tap : 5 + tap + rows, :cols]
    half = 0.5 * mixture
    return half + half * jnp.tanh(half)


def conv_state_kernel(
    x_ref, bc_ref, tail_ref, tail_bc_ref, w_ref, w_bc_ref, end_ref,
    values_ref, bc_out_ref, state_ref, joined, b_t,
):
    @pl.when(pl.program_id(0) == 0)
    def _():
        bc = filtered(bc_ref, tail_bc_ref, w_bc_ref, joined)
        bc_out_ref[...] = bc.astype(bf16)
        b_t[...] = bc[:, :STATE_DIM].T.astype(bf16)

    values = filtered(x_ref, tail_ref, w_ref, joined).astype(bf16)
    values_ref[...] = values
    scaled = jnp.concatenate(
        [
            (
                end_ref[0, :, k : k + 1]
                * values[:, k * HEAD_DIM : (k + 1) * HEAD_DIM].astype(f32)
            ).astype(bf16)
            for k in range(HEAD_BLOCK)
        ],
        axis=1,
    )
    state_ref[...] = jnp.dot(b_t[...], scaled, preferred_element_type=f32).astype(bf16)


def conv_state(xbc, tail, conv_weight, weight_end):
    rows = xbc.shape[0]
    steps = INNER // COLS
    bc_cols = 2 * STATE_DIM
    bc_at = INNER // bc_cols
    return pl.pallas_call(
        conv_state_kernel,
        grid=(steps,),
        in_specs=[
            pl.BlockSpec((rows, COLS), lambda i: (0, i)),
            pl.BlockSpec((rows, bc_cols), lambda i: (0, bc_at)),
            pl.BlockSpec((8, COLS), lambda i: (0, i)),
            pl.BlockSpec((8, bc_cols), lambda i: (0, bc_at)),
            pl.BlockSpec((4, COLS), lambda i: (0, i)),
            pl.BlockSpec((4, bc_cols), lambda i: (0, bc_at)),
            pl.BlockSpec((1, rows, HEAD_BLOCK), lambda i: (i, 0, 0)),
        ],
        out_specs=[
            pl.BlockSpec((rows, COLS), lambda i: (0, i)),
            pl.BlockSpec((rows, bc_cols), lambda i: (0, 0)),
            pl.BlockSpec((STATE_DIM, COLS), lambda i: (0, i)),
        ],
        out_shape=[
            jax.ShapeDtypeStruct((rows, INNER), bf16),
            jax.ShapeDtypeStruct((rows, bc_cols), bf16),
            jax.ShapeDtypeStruct((STATE_DIM, INNER), bf16),
        ],
        scratch_shapes=[
            pltpu.VMEM((rows + 8, COLS), f32),
            pltpu.VMEM((STATE_DIM, rows), bf16),
        ],
        compiler_params=params(),
        cost_estimate=cost(600_000_000, 11_000_000, 2_200_000),
    )(xbc, xbc, tail, tail, conv_weight, conv_weight, weight_end)


def relay_kernel(parents, held_ref, decay_ref, sent_ref):
    slot = pl.program_id(0)
    parent = parents[slot]
    grand = parents[parent]
    local = held_ref[parent].astype(f32)
    above = held_ref[grand].astype(f32)
    decay = jnp.where(grand == parent, 0.0, 1.0) * decay_ref[parent]
    end = local + decay * above
    sent_ref[0] = jnp.where(parent == slot, 0.0, end).astype(bf16)


def relay_select(parents, held, decays):
    count, rows, cols = held.shape
    return pl.pallas_call(
        relay_kernel,
        grid_spec=pltpu.PrefetchScalarGridSpec(
            num_scalar_prefetch=1,
            grid=(count,),
            in_specs=[
                pl.BlockSpec((count, rows, cols), lambda i, p: (0, 0, 0)),
                pl.BlockSpec((count, 1, cols), lambda i, p: (0, 0, 0)),
            ],
            out_specs=pl.BlockSpec((1, rows, cols), lambda i, p: (i, 0, 0)),
        ),
        out_shape=jax.ShapeDtypeStruct(held.shape, bf16),
        compiler_params=params(),
        cost_estimate=cost(4_000_000, 5_000_000),
    )(parents, held, decays)


def pick_kernel(parents, held_ref, sent_ref):
    def one(slot, carry):
        parent = parents[slot]
        sent_ref[slot, 0] = held_ref[parent]
        sent_ref[slot, 1] = held_ref[parents[parent]]
        return carry

    lax.fori_loop(0, held_ref.shape[0], one, 0)


def pick_pairs(parents, held):
    count, rows, cols = held.shape
    return pl.pallas_call(
        pick_kernel,
        grid_spec=pltpu.PrefetchScalarGridSpec(
            num_scalar_prefetch=1,
            grid=(1,),
            in_specs=[pl.BlockSpec((count, rows, cols), lambda i, p: (0, 0, 0))],
            out_specs=pl.BlockSpec((count, 2, rows, cols), lambda i, p: (0, 0, 0, 0)),
        ),
        out_shape=jax.ShapeDtypeStruct((count, 2, rows, cols), bf16),
        compiler_params=params(),
        cost_estimate=cost(0, 1_500_000),
    )(parents, held)


NT = (((1,), (1,)), ((), ()))


def attend_kernel(depth_ref, q_ref, ko, vo, kp, vp, kg, vg, out_ref):
    rows = q_ref.shape[0]
    depth = depth_ref[0]
    parent_bias = jnp.where(depth >= 1, 0.0, FAR)
    grand_bias = jnp.where(depth >= 2, 0.0, FAR)
    row = lax.broadcasted_iota(jnp.int32, (rows, rows), 0)
    col = lax.broadcasted_iota(jnp.int32, (rows, rows), 1)
    own_side = col <= row
    rate = ATT_DIM ** (-0.5) * LOG2E
    keys_own, keys_parent, keys_grand = ko[...], kp[...], kg[...]
    values_own, values_parent, values_grand = vo[...], vp[...], vg[...]
    for g in range(q_ref.shape[1] // ATT_DIM):
        at = slice(g * ATT_DIM, (g + 1) * ATT_DIM)
        q = q_ref[:, at]
        own = lax.dot_general(q, keys_own, NT, preferred_element_type=f32)
        grand = lax.dot_general(q, keys_grand, NT, preferred_element_type=f32)
        parent = lax.dot_general(q, keys_parent, NT, preferred_element_type=f32) + parent_bias
        mixed = jnp.where(own_side, own, grand + grand_bias)
        peak = jnp.max(jnp.maximum(mixed, parent), axis=1, keepdims=True)
        mixed = jnp.exp2((mixed - peak) * rate)
        parent = jnp.exp2((parent - peak) * rate)
        total = jnp.sum(mixed + parent, axis=1, keepdims=True)
        own = jnp.where(own_side, mixed, 0.0).astype(bf16)
        grand = jnp.where(own_side, 0.0, mixed).astype(bf16)
        out = jnp.dot(own, values_own, preferred_element_type=f32)
        out += jnp.dot(parent.astype(bf16), values_parent, preferred_element_type=f32)
        out += jnp.dot(grand, values_grand, preferred_element_type=f32)
        out_ref[:, at] = (out * (1.0 / total)).astype(bf16)


def attend(depth, queries, own, parent, grand):
    rows, width = queries.shape
    block = width // KV_HEADS
    key = pl.BlockSpec((rows, ATT_DIM), lambda i, d: (0, i))
    value = pl.BlockSpec((rows, ATT_DIM), lambda i, d: (0, KV_HEADS + i))
    return pl.pallas_call(
        attend_kernel,
        grid_spec=pltpu.PrefetchScalarGridSpec(
            num_scalar_prefetch=1,
            grid=(KV_HEADS,),
            in_specs=[pl.BlockSpec((rows, block), lambda i, d: (0, i))] + [key, value] * 3,
            out_specs=pl.BlockSpec((rows, block), lambda i, d: (0, i)),
        ),
        out_shape=jax.ShapeDtypeStruct(queries.shape, bf16),
        compiler_params=params(),
        cost_estimate=cost(3_300_000_000, 6_000_000, 4_200_000),
    )(depth, queries, own, own, parent, parent, grand, grand)


def intra_kernel(values_ref, bc_ref, cum_ref, gap_ref, gain_ref, out_ref, scores):
    rows = values_ref.shape[0]
    row = lax.broadcasted_iota(jnp.int32, (rows, rows), 0)
    col = lax.broadcasted_iota(jnp.int32, (rows, rows), 1)
    causal = col <= row

    @pl.when(pl.program_id(0) == 0)
    def _():
        scores[...] = lax.dot_general(
            bc_ref[:, STATE_DIM:], bc_ref[:, :STATE_DIM], NT, preferred_element_type=f32
        )

    for k in range(HEAD_BLOCK):
        at = slice(k * HEAD_DIM, (k + 1) * HEAD_DIM)
        power = jnp.where(causal, cum_ref[0, :, k : k + 1] - gap_ref[k : k + 1, :], FAR)
        kernel = (scores[...] * jnp.exp2(power)).astype(bf16)
        values = values_ref[:, at]
        out = jnp.dot(kernel, values, preferred_element_type=f32)
        out_ref[:, at] = out + gain_ref[:, at] * values.astype(f32)


def intra(values, bc, cum2, gap2, gain):
    rows = values.shape[0]
    wide = pl.BlockSpec((rows, COLS), lambda i: (0, i))
    return pl.pallas_call(
        intra_kernel,
        grid=(INNER // COLS,),
        in_specs=[
            wide,
            pl.BlockSpec((rows, 2 * STATE_DIM), lambda i: (0, 0)),
            pl.BlockSpec((1, rows, HEAD_BLOCK), lambda i: (i, 0, 0)),
            pl.BlockSpec((HEAD_BLOCK, rows), lambda i: (i, 0)),
            pl.BlockSpec((1, COLS), lambda i: (0, i)),
        ],
        out_specs=wide,
        out_shape=jax.ShapeDtypeStruct((rows, INNER), f32),
        scratch_shapes=[pltpu.VMEM((rows, rows), f32)],
        compiler_params=params(),
        cost_estimate=cost(1_100_000_000, 12_600_000, 4_200_000),
    )(values, bc, cum2, gap2, gain)


def finish_kernel(intra_ref, c_ref, initial_ref, grow_ref, out_ref, summed, squares):
    step = pl.program_id(0)
    last = pl.num_programs(0) - 1
    carried = jnp.dot(c_ref[...], initial_ref[...], preferred_element_type=f32)
    mixer = intra_ref[...] + jnp.concatenate(
        [
            grow_ref[0, :, k : k + 1] * carried[:, k * HEAD_DIM : (k + 1) * HEAD_DIM]
            for k in range(HEAD_BLOCK)
        ],
        axis=1,
    )
    square = mixer * mixer
    part = square[:, :HEAD_DIM]
    for k in range(1, HEAD_BLOCK):
        part += square[:, k * HEAD_DIM : (k + 1) * HEAD_DIM]
    summed[step] = mixer
    squares[...] = jnp.where(step == 0, part, squares[...] + part)

    @pl.when(step == last)
    def _():
        mean = jnp.sum(squares[...], axis=1, keepdims=True) * (1.0 / INNER)
        scale = lax.rsqrt(mean + EPSILON)
        for s in range(INNER // COLS):
            out_ref[:, s * COLS : (s + 1) * COLS] = (summed[s] * scale).astype(bf16)


def finish(intra_rows, bc, initial, grow):
    rows = intra_rows.shape[0]
    steps = INNER // COLS
    return pl.pallas_call(
        finish_kernel,
        grid=(steps,),
        in_specs=[
            pl.BlockSpec((rows, COLS), lambda i: (0, i)),
            pl.BlockSpec((rows, STATE_DIM), lambda i: (0, 1)),
            pl.BlockSpec((STATE_DIM, COLS), lambda i: (0, i)),
            pl.BlockSpec((1, rows, HEAD_BLOCK), lambda i: (i, 0, 0)),
        ],
        out_specs=pl.BlockSpec((rows, INNER), lambda i: (0, 0)),
        out_shape=jax.ShapeDtypeStruct((rows, INNER), bf16),
        scratch_shapes=[
            pltpu.VMEM((steps, rows, COLS), f32),
            pltpu.VMEM((rows, HEAD_DIM), f32),
        ],
        compiler_params=params(),
        cost_estimate=cost(600_000_000, 14_600_000),
    )(intra_rows, bc, initial, grow)


def prefix_sum(terms):
    rows = terms.shape[0]
    lower = (jnp.arange(rows)[:, None] >= jnp.arange(rows)[None, :]).astype(f32)
    return jnp.dot(lower, terms, precision=lax.Precision.HIGHEST, preferred_element_type=f32)


def by_block(columns):
    rows, heads = columns.shape
    return columns.reshape(rows, heads // HEAD_BLOCK, HEAD_BLOCK).transpose(1, 0, 2)


def exchange(rows):
    return lax.all_to_all(rows, "branch", split_axis=0, concat_axis=0, tiled=True)


def on_device(
    xbc, step_size, queries, keys_values, parent_slot, decay_rate, skip_gain, conv_weight
):
    count = lax.axis_size("branch")
    me = lax.axis_index("branch")
    rows = xbc.shape[0]
    taps = conv_weight.shape[0] - 1
    my_parent = parent_slot[me]
    my_grand = parent_slot[my_parent]
    is_root = my_parent == me
    depth = jnp.where(is_root, 0, jnp.where(my_grand == my_parent, 1, 2)).astype(jnp.int32)

    cumulative = prefix_sum(-decay_rate[None, :] * step_size)
    last = cumulative[-1:]
    weight_end = by_block(jnp.exp(last - cumulative) * step_size)
    fall = jnp.exp(-decay_rate * jnp.sum(step_size, axis=0))
    high = lax.reduce_precision(fall, 8, 7)
    parts = jnp.concatenate([high, fall - high]).astype(bf16)
    parts = jnp.broadcast_to(parts[None], (taps, parts.shape[0]))
    sent = jnp.concatenate([xbc[rows - taps :], parts], axis=1)
    gathered = lax.all_gather(sent, "branch")
    held_pairs = exchange(keys_values.reshape(count, rows // count, -1))
    sent_pairs = pick_pairs(parent_slot, held_pairs)
    width = xbc.shape[1]
    tails = gathered[:, :, :width]
    decays = gathered[:, :1, width : width + SSM_HEADS].astype(f32)
    decays += gathered[:, :1, width + SSM_HEADS :].astype(f32)
    decays = jnp.broadcast_to(decays[:, :, :, None], (count, 1, SSM_HEADS, HEAD_DIM))
    decays = decays.reshape(count, 1, INNER)
    grow = by_block(jnp.exp(cumulative))
    cum2 = by_block(cumulative * LOG2E)
    gap2 = ((cumulative - jnp.log(step_size)) * LOG2E).T
    gain = jnp.broadcast_to(skip_gain[:, None], (SSM_HEADS, HEAD_DIM)).reshape(1, INNER)

    tail = lax.dynamic_index_in_dim(tails, my_parent, 0, keepdims=False).astype(f32)
    tail = jnp.where(is_root, 0.0, tail)
    tail = jnp.concatenate([jnp.zeros((8 - taps, tail.shape[1]), f32), tail], axis=0)
    tail, sent_pairs = lax.optimization_barrier((tail, sent_pairs))
    pairs = exchange(sent_pairs)
    values, bc, state = conv_state(xbc, tail, conv_weight, weight_end)

    state, pairs = lax.optimization_barrier((state, pairs))
    held = exchange(state.reshape(count, STATE_DIM // count, INNER))
    intra_rows = intra(values, bc, cum2, gap2, gain)
    held, intra_rows = lax.optimization_barrier((held, intra_rows))
    initial = exchange(relay_select(parent_slot, held, decays)).reshape(STATE_DIM, INNER)

    parent_pairs = pairs[:, 0].reshape(rows, -1)
    grand_pairs = pairs[:, 1].reshape(rows, -1)
    attended = attend(depth[None], queries, keys_values, parent_pairs, grand_pairs)
    attended, intra_rows = lax.optimization_barrier((attended, intra_rows))
    return (finish(intra_rows, bc, initial, grow), attended)


def solution(mesh):
    rows = P(("groups", "branch"), None)
    in_specs = (rows, rows, rows, rows, P("groups"), P(), P(), P())
    return jax.shard_map(
        on_device, mesh=mesh, in_specs=in_specs, out_specs=(rows, rows), check_vma=False
    )
```

```python
import math

import jax
import jax.numpy as jnp
from jax import lax
from jax.experimental import pallas as pl
from jax.experimental.pallas import tpu as pltpu
from jax.sharding import PartitionSpec as P

SSM_HEADS = 64
HEAD_DIM = 128
STATE_DIM = 128
Q_HEADS = 32
KV_HEADS = 4
ATT_DIM = 128
INNER = SSM_HEADS * HEAD_DIM
EPSILON = 1e-05
LOG2E = math.log2(math.e)
FAR = -1e30
HEAD_BLOCK = 8
COLS = HEAD_BLOCK * HEAD_DIM
VMEM_LIMIT = 50 * 1024 * 1024
bf16, f32 = jnp.bfloat16, jnp.float32


def params():
    return pltpu.CompilerParams(vmem_limit_bytes=VMEM_LIMIT)


def cost(flops, moved, transcendentals=0):
    return pl.CostEstimate(flops=flops, bytes_accessed=moved, transcendentals=transcendentals)


def filtered(x_ref, tail_ref, weight_ref, joined):
    rows, cols = x_ref.shape
    joined[0:8, :cols] = tail_ref[...]
    joined[8 : 8 + rows, :cols] = x_ref[...].astype(f32)
    mixture = weight_ref[3:4, :] * joined[8 : 8 + rows, :cols]
    for tap in range(3):
        mixture += weight_ref[tap : tap + 1, :] * joined[5 + tap : 5 + tap + rows, :cols]
    half = 0.5 * mixture
    return half + half * jnp.tanh(half)


def conv_state_kernel(
    x_ref, bc_ref, tail_ref, tail_bc_ref, w_ref, w_bc_ref, end_ref,
    values_ref, bc_out_ref, state_ref, joined, b_t,
):
    @pl.when(pl.program_id(0) == 0)
    def _():
        bc = filtered(bc_ref, tail_bc_ref, w_bc_ref, joined)
        bc_out_ref[...] = bc.astype(bf16)
        b_t[...] = bc[:, :STATE_DIM].T.astype(bf16)

    values = filtered(x_ref, tail_ref, w_ref, joined).astype(bf16)
    values_ref[...] = values
    scaled = jnp.concatenate(
        [
            (
                end_ref[0, :, k : k + 1]
                * values[:, k * HEAD_DIM : (k + 1) * HEAD_DIM].astype(f32)
            ).astype(bf16)
            for k in range(HEAD_BLOCK)
        ],
        axis=1,
    )
    state_ref[...] = jnp.dot(b_t[...], scaled, preferred_element_type=f32).astype(bf16)


def conv_state(xbc, tail, conv_weight, weight_end):
    rows = xbc.shape[0]
    steps = INNER // COLS
    bc_cols = 2 * STATE_DIM
    bc_at = INNER // bc_cols
    return pl.pallas_call(
        conv_state_kernel,
        grid=(steps,),
        in_specs=[
            pl.BlockSpec((rows, COLS), lambda i: (0, i)),
            pl.BlockSpec((rows, bc_cols), lambda i: (0, bc_at)),
            pl.BlockSpec((8, COLS), lambda i: (0, i)),
            pl.BlockSpec((8, bc_cols), lambda i: (0, bc_at)),
            pl.BlockSpec((4, COLS), lambda i: (0, i)),
            pl.BlockSpec((4, bc_cols), lambda i: (0, bc_at)),
            pl.BlockSpec((1, rows, HEAD_BLOCK), lambda i: (i, 0, 0)),
        ],
        out_specs=[
            pl.BlockSpec((rows, COLS), lambda i: (0, i)),
            pl.BlockSpec((rows, bc_cols), lambda i: (0, 0)),
            pl.BlockSpec((STATE_DIM, COLS), lambda i: (0, i)),
        ],
        out_shape=[
            jax.ShapeDtypeStruct((rows, INNER), bf16),
            jax.ShapeDtypeStruct((rows, bc_cols), bf16),
            jax.ShapeDtypeStruct((STATE_DIM, INNER), bf16),
        ],
        scratch_shapes=[
            pltpu.VMEM((rows + 8, COLS), f32),
            pltpu.VMEM((STATE_DIM, rows), bf16),
        ],
        compiler_params=params(),
        cost_estimate=cost(600_000_000, 11_000_000, 2_200_000),
    )(xbc, xbc, tail, tail, conv_weight, conv_weight, weight_end)


def relay_kernel(parents, held_ref, decay_ref, sent_ref):
    slot = pl.program_id(0)
    parent = parents[slot]
    grand = parents[parent]
    local = held_ref[parent].astype(f32)
    above = held_ref[grand].astype(f32)
    decay = jnp.where(grand == parent, 0.0, 1.0) * decay_ref[parent]
    end = local + decay * above
    sent_ref[0] = jnp.where(parent == slot, 0.0, end).astype(bf16)


def relay_select(parents, held, decays):
    count, rows, cols = held.shape
    return pl.pallas_call(
        relay_kernel,
        grid_spec=pltpu.PrefetchScalarGridSpec(
            num_scalar_prefetch=1,
            grid=(count,),
            in_specs=[
                pl.BlockSpec((count, rows, cols), lambda i, p: (0, 0, 0)),
                pl.BlockSpec((count, 1, cols), lambda i, p: (0, 0, 0)),
            ],
            out_specs=pl.BlockSpec((1, rows, cols), lambda i, p: (i, 0, 0)),
        ),
        out_shape=jax.ShapeDtypeStruct(held.shape, bf16),
        compiler_params=params(),
        cost_estimate=cost(4_000_000, 5_000_000),
    )(parents, held, decays)


def pick_kernel(parents, held_ref, sent_ref):
    def one(slot, carry):
        parent = parents[slot]
        sent_ref[slot, 0] = held_ref[parent]
        sent_ref[slot, 1] = held_ref[parents[parent]]
        return carry

    lax.fori_loop(0, held_ref.shape[0], one, 0)


def pick_pairs(parents, held):
    count, rows, cols = held.shape
    return pl.pallas_call(
        pick_kernel,
        grid_spec=pltpu.PrefetchScalarGridSpec(
            num_scalar_prefetch=1,
            grid=(1,),
            in_specs=[pl.BlockSpec((count, rows, cols), lambda i, p: (0, 0, 0))],
            out_specs=pl.BlockSpec((count, 2, rows, cols), lambda i, p: (0, 0, 0, 0)),
        ),
        out_shape=jax.ShapeDtypeStruct((count, 2, rows, cols), bf16),
        compiler_params=params(),
        cost_estimate=cost(0, 1_500_000),
    )(parents, held)


NT = (((1,), (1,)), ((), ()))


def attend_kernel(depth_ref, q_ref, ko, vo, kp, vp, kg, vg, out_ref):
    rows = q_ref.shape[0]
    depth = depth_ref[0]
    parent_bias = jnp.where(depth >= 1, 0.0, FAR)
    grand_bias = jnp.where(depth >= 2, 0.0, FAR)
    row = lax.broadcasted_iota(jnp.int32, (rows, rows), 0)
    col = lax.broadcasted_iota(jnp.int32, (rows, rows), 1)
    own_side = col <= row
    rate = ATT_DIM ** (-0.5) * LOG2E
    keys_own, keys_parent, keys_grand = ko[...], kp[...], kg[...]
    values_own, values_parent, values_grand = vo[...], vp[...], vg[...]
    for g in range(q_ref.shape[1] // ATT_DIM):
        at = slice(g * ATT_DIM, (g + 1) * ATT_DIM)
        q = q_ref[:, at]
        own = lax.dot_general(q, keys_own, NT, preferred_element_type=f32)
        grand = lax.dot_general(q, keys_grand, NT, preferred_element_type=f32)
        parent = lax.dot_general(q, keys_parent, NT, preferred_element_type=f32) + parent_bias
        mixed = jnp.where(own_side, own, grand + grand_bias)
        peak = jnp.max(jnp.maximum(mixed, parent), axis=1, keepdims=True)
        mixed = jnp.exp2((mixed - peak) * rate)
        parent = jnp.exp2((parent - peak) * rate)
        total = jnp.sum(mixed + parent, axis=1, keepdims=True)
        own = jnp.where(own_side, mixed, 0.0).astype(bf16)
        grand = jnp.where(own_side, 0.0, mixed).astype(bf16)
        out = jnp.dot(own, values_own, preferred_element_type=f32)
        out += jnp.dot(parent.astype(bf16), values_parent, preferred_element_type=f32)
        out += jnp.dot(grand, values_grand, preferred_element_type=f32)
        out_ref[:, at] = (out * (1.0 / total)).astype(bf16)


def attend(depth, queries, own, parent, grand):
    rows, width = queries.shape
    block = width // KV_HEADS
    key = pl.BlockSpec((rows, ATT_DIM), lambda i, d: (0, i))
    value = pl.BlockSpec((rows, ATT_DIM), lambda i, d: (0, KV_HEADS + i))
    return pl.pallas_call(
        attend_kernel,
        grid_spec=pltpu.PrefetchScalarGridSpec(
            num_scalar_prefetch=1,
            grid=(KV_HEADS,),
            in_specs=[pl.BlockSpec((rows, block), lambda i, d: (0, i))] + [key, value] * 3,
            out_specs=pl.BlockSpec((rows, block), lambda i, d: (0, i)),
        ),
        out_shape=jax.ShapeDtypeStruct(queries.shape, bf16),
        compiler_params=params(),
        cost_estimate=cost(3_300_000_000, 6_000_000, 4_200_000),
    )(depth, queries, own, own, parent, parent, grand, grand)


def intra_kernel(values_ref, bc_ref, cum_ref, gap_ref, gain_ref, out_ref, scores):
    rows = values_ref.shape[0]
    row = lax.broadcasted_iota(jnp.int32, (rows, rows), 0)
    col = lax.broadcasted_iota(jnp.int32, (rows, rows), 1)
    causal = col <= row

    @pl.when(pl.program_id(0) == 0)
    def _():
        scores[...] = lax.dot_general(
            bc_ref[:, STATE_DIM:], bc_ref[:, :STATE_DIM], NT, preferred_element_type=f32
        )

    for k in range(HEAD_BLOCK):
        at = slice(k * HEAD_DIM, (k + 1) * HEAD_DIM)
        power = jnp.where(causal, cum_ref[0, :, k : k + 1] - gap_ref[k : k + 1, :], FAR)
        kernel = (scores[...] * jnp.exp2(power)).astype(bf16)
        values = values_ref[:, at]
        out = jnp.dot(kernel, values, preferred_element_type=f32)
        out_ref[:, at] = out + gain_ref[:, at] * values.astype(f32)


def intra(values, bc, cum2, gap2, gain):
    rows = values.shape[0]
    wide = pl.BlockSpec((rows, COLS), lambda i: (0, i))
    return pl.pallas_call(
        intra_kernel,
        grid=(INNER // COLS,),
        in_specs=[
            wide,
            pl.BlockSpec((rows, 2 * STATE_DIM), lambda i: (0, 0)),
            pl.BlockSpec((1, rows, HEAD_BLOCK), lambda i: (i, 0, 0)),
            pl.BlockSpec((HEAD_BLOCK, rows), lambda i: (i, 0)),
            pl.BlockSpec((1, COLS), lambda i: (0, i)),
        ],
        out_specs=wide,
        out_shape=jax.ShapeDtypeStruct((rows, INNER), f32),
        scratch_shapes=[pltpu.VMEM((rows, rows), f32)],
        compiler_params=params(),
        cost_estimate=cost(1_100_000_000, 12_600_000, 4_200_000),
    )(values, bc, cum2, gap2, gain)


def finish_kernel(intra_ref, c_ref, initial_ref, grow_ref, out_ref, summed, squares):
    step = pl.program_id(0)
    last = pl.num_programs(0) - 1
    carried = jnp.dot(c_ref[...], initial_ref[...], preferred_element_type=f32)
    mixer = intra_ref[...] + jnp.concatenate(
        [
            grow_ref[0, :, k : k + 1] * carried[:, k * HEAD_DIM : (k + 1) * HEAD_DIM]
            for k in range(HEAD_BLOCK)
        ],
        axis=1,
    )
    square = mixer * mixer
    part = square[:, :HEAD_DIM]
    for k in range(1, HEAD_BLOCK):
        part += square[:, k * HEAD_DIM : (k + 1) * HEAD_DIM]
    summed[step] = mixer
    squares[...] = jnp.where(step == 0, part, squares[...] + part)

    @pl.when(step == last)
    def _():
        mean = jnp.sum(squares[...], axis=1, keepdims=True) * (1.0 / INNER)
        scale = lax.rsqrt(mean + EPSILON)
        for s in range(INNER // COLS):
            out_ref[:, s * COLS : (s + 1) * COLS] = (summed[s] * scale).astype(bf16)


def finish(intra_rows, bc, initial, grow):
    rows = intra_rows.shape[0]
    steps = INNER // COLS
    return pl.pallas_call(
        finish_kernel,
        grid=(steps,),
        in_specs=[
            pl.BlockSpec((rows, COLS), lambda i: (0, i)),
            pl.BlockSpec((rows, STATE_DIM), lambda i: (0, 1)),
            pl.BlockSpec((STATE_DIM, COLS), lambda i: (0, i)),
            pl.BlockSpec((1, rows, HEAD_BLOCK), lambda i: (i, 0, 0)),
        ],
        out_specs=pl.BlockSpec((rows, INNER), lambda i: (0, 0)),
        out_shape=jax.ShapeDtypeStruct((rows, INNER), bf16),
        scratch_shapes=[
            pltpu.VMEM((steps, rows, COLS), f32),
            pltpu.VMEM((rows, HEAD_DIM), f32),
        ],
        compiler_params=params(),
        cost_estimate=cost(600_000_000, 14_600_000),
    )(intra_rows, bc, initial, grow)


def prefix_sum(terms):
    rows = terms.shape[0]
    lower = (jnp.arange(rows)[:, None] >= jnp.arange(rows)[None, :]).astype(f32)
    return jnp.dot(lower, terms, precision=lax.Precision.HIGHEST, preferred_element_type=f32)


def by_block(columns):
    rows, heads = columns.shape
    return columns.reshape(rows, heads // HEAD_BLOCK, HEAD_BLOCK).transpose(1, 0, 2)


def exchange(rows):
    return lax.all_to_all(rows, "branch", split_axis=0, concat_axis=0, tiled=True)


def on_device(
    xbc, step_size, queries, keys_values, parent_slot, decay_rate, skip_gain, conv_weight
):
    count = lax.axis_size("branch")
    me = lax.axis_index("branch")
    rows = xbc.shape[0]
    taps = conv_weight.shape[0] - 1
    my_parent = parent_slot[me]
    my_grand = parent_slot[my_parent]
    is_root = my_parent == me
    depth = jnp.where(is_root, 0, jnp.where(my_grand == my_parent, 1, 2)).astype(jnp.int32)

    cumulative = prefix_sum(-decay_rate[None, :] * step_size)
    last = cumulative[-1:]
    weight_end = by_block(jnp.exp(last - cumulative) * step_size)
    fall = jnp.exp(-decay_rate * jnp.sum(step_size, axis=0))
    high = lax.reduce_precision(fall, 8, 7)
    parts = jnp.concatenate([high, fall - high]).astype(bf16)
    pairs = keys_values.reshape(count, rows // count, -1)
    share, width = taps * xbc.shape[1] // count, pairs.shape[2]
    parts = jnp.broadcast_to(parts[None], (count, parts.shape[0]))
    extra = jnp.concatenate([xbc[rows - taps :].reshape(count, share), parts], axis=1)
    more = -(-extra.shape[1] // width)
    extra = jnp.pad(extra, ((0, 0), (0, more * width - extra.shape[1])))
    held_pairs = exchange(jnp.concatenate([pairs, extra.reshape(count, more, width)], axis=1))
    sent_pairs = pick_pairs(parent_slot, held_pairs)
    decays = held_pairs[:, rows // count :].reshape(count, 1, -1)[:, :, share : share + 2 * SSM_HEADS]
    decays = decays.astype(f32)
    decays = decays[:, :, :SSM_HEADS] + decays[:, :, SSM_HEADS:]
    decays = jnp.broadcast_to(decays[:, :, :, None], (count, 1, SSM_HEADS, HEAD_DIM))
    decays = decays.reshape(count, 1, INNER)
    grow = by_block(jnp.exp(cumulative))
    cum2 = by_block(cumulative * LOG2E)
    gap2 = ((cumulative - jnp.log(step_size)) * LOG2E).T
    gain = jnp.broadcast_to(skip_gain[:, None], (SSM_HEADS, HEAD_DIM)).reshape(1, INNER)

    pairs = exchange(sent_pairs)
    tail = pairs[:, 0, rows // count :].reshape(count, -1)[:, :share]
    tail = tail.reshape(taps, xbc.shape[1]).astype(f32)
    tail = jnp.where(is_root, 0.0, tail)
    tail = jnp.concatenate([jnp.zeros((8 - taps, tail.shape[1]), f32), tail], axis=0)
    values, bc, state = conv_state(xbc, tail, conv_weight, weight_end)

    held = exchange(state.reshape(count, STATE_DIM // count, INNER))
    intra_rows = intra(values, bc, cum2, gap2, gain)
    held, intra_rows = lax.optimization_barrier((held, intra_rows))
    initial = exchange(relay_select(parent_slot, held, decays)).reshape(STATE_DIM, INNER)

    parent_pairs = pairs[:, 0, : rows // count].reshape(rows, -1)
    grand_pairs = pairs[:, 1, : rows // count].reshape(rows, -1)
    attended = attend(depth[None], queries, keys_values, parent_pairs, grand_pairs)
    attended, intra_rows = lax.optimization_barrier((attended, intra_rows))
    return (finish(intra_rows, bc, initial, grow), attended)


def solution(mesh):
    rows = P(("groups", "branch"), None)
    in_specs = (rows, rows, rows, rows, P("groups"), P(), P(), P())
    return jax.shard_map(
        on_device, mesh=mesh, in_specs=in_specs, out_specs=(rows, rows), check_vma=False
    )
```
